256 devices in a mesh: row: 32 (over y, z), col: 8 (over x, core).
Axes of the slice: x: 4, y: 4, z: 8, core: 2. Of those that a mesh axis runs over, the one named last changes fastest.
Arguments:
- tokens: bfloat16 [256, 16384], P('row', 'col'), may hold values from -6 to 6
- gate_frozen_weight: bfloat16 [16384, 28672], P('col', 'row'), may hold values from -0.046875 to 0.046875
- up_frozen_weight: bfloat16 [16384, 28672], P('col', 'row'), may hold values from -0.046875 to 0.046875
- down_frozen_weight: bfloat16 [28672, 16384], P('row', 'col'), may hold values from -0.03125 to 0.03125
- gate_adapter_squeeze: bfloat16 [16384, 16], P('col'), may hold values from -0.046875 to 0.046875
- gate_adapter_lift: bfloat16 [16, 28672], P(None, 'row'), may hold values from -1.5 to 1.5
- up_adapter_squeeze: bfloat16 [16384, 16], P('col'), may hold values from -0.046875 to 0.046875
- up_adapter_lift: bfloat16 [16, 28672], P(None, 'row'), may hold values from -1.5 to 1.5
- down_adapter_squeeze: bfloat16 [28672, 16], P('row'), may hold values from -0.03125 to 0.03125
- down_adapter_lift: bfloat16 [16, 16384], P(None, 'col'), may hold values from -1.5 to 1.5
- output_gradient: bfloat16 [256, 16384], P('row', 'col'), may hold values from -6 to 6
Outputs:
- mixed: bfloat16 [256, 16384], P('row', 'col')
- token_gradient: bfloat16 [256, 16384], P('row', 'col')
The draws below stay inside these ranges and needn't reach their ends.
All inputs are finite; a program needn't handle non-finite values.
Results may differ from the reference program's by a relative error of at most 0.005.
Values may be sent and summed in bfloat16 or wider, within the bound.
A program may use at most 64 MiB of HBM per device.

```python
import jax
import jax.numpy as jnp
from jax import lax

D = 16384
FF = 28672
RANK = 16
TOKENS = 256


def block_scale(key, shape, shards, smallest, high):
    gain = 1.0
    for axis_at, shards_of in shards:
        heights = jax.random.uniform(jax.random.fold_in(jax.random.fold_in(key, 6), axis_at), (shards_of,), jnp.float32, smallest / len(shards), high / len(shards))
        gain = gain * jnp.repeat(jnp.exp(heights), shape[axis_at] // shards_of).reshape((-1,) + (1,) * (len(shape) - 1 - axis_at))
    return gain


def scatter_about(stream_key, shape, spread, bound, shards=(), dtype=jnp.bfloat16):
    entries = jax.random.normal(stream_key, shape, jnp.float32) * spread
    if len(shards) > 0:
        entries = block_scale(stream_key, shape, shards, -0.22, 0.18) * entries
    return jnp.clip(entries, min=-bound, max=bound).astype(dtype)


def setup_inputs(seed: int = 0) -> dict:
    seeds = jax.random.split(jax.random.key(seed), 12)
    return {
        "tokens": scatter_about(seeds[0], (TOKENS, D), 1.0, 6.0, ((0, 32), (1, 8))),
        "gate_frozen_weight": scatter_about(seeds[1], (D, FF), D ** -0.5, 0.046875, ((0, 8), (1, 32))),
        "up_frozen_weight": scatter_about(seeds[2], (D, FF), D ** -0.5, 0.046875, ((0, 8), (1, 32))),
        "down_frozen_weight": scatter_about(seeds[3], (FF, D), FF ** -0.5, 0.03125, ((0, 32), (1, 8))),
        "gate_adapter_squeeze": scatter_about(seeds[4], (D, RANK), D ** -0.5, 0.046875, ((0, 8),)),
        "gate_adapter_lift": scatter_about(seeds[5], (RANK, FF), 0.25, 1.5, ((1, 32),)),
        "up_adapter_squeeze": scatter_about(seeds[6], (D, RANK), D ** -0.5, 0.046875, ((0, 8),)),
        "up_adapter_lift": scatter_about(seeds[7], (RANK, FF), 0.25, 1.5, ((1, 32),)),
        "down_adapter_squeeze": scatter_about(seeds[8], (FF, RANK), FF ** -0.5, 0.03125, ((0, 32),)),
        "down_adapter_lift": scatter_about(seeds[9], (RANK, D), 0.25, 1.5, ((1, 8),)),
        "output_gradient": scatter_about(seeds[10], (TOKENS, D), 1.0, 6.0, ((0, 32), (1, 8))),
    }


ADAPTER_SCALE = 0.5


def adapter_contribution(left, project, expand):
    inner = jnp.dot(left, project, preferred_element_type=jnp.float32)
    return jnp.dot(inner, expand.astype(jnp.float32), precision=lax.Precision.HIGHEST)


def adapter_transposed(left, expand, project):
    inner = jnp.dot(left, expand.T, preferred_element_type=jnp.float32)
    return jnp.dot(inner, project.T.astype(jnp.float32), precision=lax.Precision.HIGHEST)


def reference(tokens, gate_frozen_weight, up_frozen_weight, down_frozen_weight, gate_adapter_squeeze, gate_adapter_lift, up_adapter_squeeze, up_adapter_lift, down_adapter_squeeze, down_adapter_lift, output_gradient):
    gate_complete = jnp.dot(tokens, gate_frozen_weight, preferred_element_type=jnp.float32) + ADAPTER_SCALE * adapter_contribution(tokens, gate_adapter_squeeze, gate_adapter_lift)
    up_complete = jnp.dot(tokens, up_frozen_weight, preferred_element_type=jnp.float32) + ADAPTER_SCALE * adapter_contribution(tokens, up_adapter_squeeze, up_adapter_lift)
    sigmoid_gate = jax.nn.sigmoid(gate_complete)
    hidden_activation = (gate_complete * sigmoid_gate * up_complete).astype(jnp.bfloat16)
    mixed = jnp.dot(hidden_activation, down_frozen_weight, preferred_element_type=jnp.float32) + ADAPTER_SCALE * adapter_contribution(hidden_activation, down_adapter_squeeze, down_adapter_lift)
    hidden_gradient = jnp.dot(output_gradient, down_frozen_weight.T, preferred_element_type=jnp.float32) + ADAPTER_SCALE * adapter_transposed(output_gradient, down_adapter_lift, down_adapter_squeeze)
    gate_gradient = (hidden_gradient * up_complete * sigmoid_gate * (1.0 + gate_complete * (1.0 - sigmoid_gate))).astype(jnp.bfloat16)
    up_gradient = (hidden_gradient * gate_complete * sigmoid_gate).astype(jnp.bfloat16)
    token_gradient = jnp.dot(gate_gradient, gate_frozen_weight.T, preferred_element_type=jnp.float32) + jnp.dot(up_gradient, up_frozen_weight.T, preferred_element_type=jnp.float32)
    token_gradient = token_gradient + ADAPTER_SCALE * (adapter_transposed(gate_gradient, gate_adapter_lift, gate_adapter_squeeze) + adapter_transposed(up_gradient, up_adapter_lift, up_adapter_squeeze))
    return mixed.astype(jnp.bfloat16), token_gradient.astype(jnp.bfloat16)
```

```python
import jax
import jax.numpy as jnp
from jax import lax
from jax.experimental import pallas as pl
from jax.experimental.pallas import tpu as pltpu
from jax.sharding import PartitionSpec as P

MESH = pl.DeviceIdType.MESH
F32, BF16 = jnp.float32, jnp.bfloat16

NX, NCORE, NY, NZ = 4, 2, 4, 8
T, DC, FR, RANK = 256, 2048, 896, 16
FA = 1024
HALF, QUART = T // NCORE, T // NCORE // NX
TY = T // NY
CW = 512
NCH = DC // CW
ZORD = (1, 7, 2, 6, 3, 5, 4)
YORD = (1, 3, 2)
SCALE = 0.5


def nn(a, b):
    return jnp.dot(a, b, preferred_element_type=F32)


def nt(a, b):
    return lax.dot_general(a, b, (((1,), (1,)), ((), ())), preferred_element_type=F32)


def split_inner(inner):
    top = inner.astype(BF16).astype(F32)
    lane = lax.broadcasted_iota(jnp.int32, inner.shape, 1)
    return (jnp.where(lane < RANK, top, inner - top) * SCALE).astype(BF16)


def kernel(
    x_ref, dy_ref, wg_ref, wu_ref, wd_ref, sg_ref, lg_ref, su_ref, lu_ref, sd_ref, ld_ref,
    mixed_ref, tg_ref,
    wga, wua, wda, lga, lua, sda, sgt, sut, sdt,
    g, pan, part, sib, own, xs, xr, act, mf, ms, ry, zo, zs, zr,
    wsem, ss, rs,
):
    r, c = lax.axis_index("row"), lax.axis_index("col")
    y, z = r // NZ, r % NZ
    x, k = c // NCORE, c % NCORE

    def dev(dx=0, dk=0, dy=0, dz=0):
        return {
            "row": ((y + dy) % NY) * NZ + (z + dz) % NZ,
            "col": ((x + dx) % NX) * NCORE + (k + dk) % NCORE,
        }

    peers = (
        [dict(dz=d) for d in range(1, NZ)]
        + [dict(dy=d) for d in range(1, NY)]
        + [dict(dx=d) for d in range(1, NX)]
        + [dict(dk=1)]
    )
    barrier = pltpu.get_barrier_semaphore()
    for p in peers:
        pl.semaphore_signal(barrier, inc=1, device_id=dev(**p), device_id_type=MESH)

    loads = {}

    def load(name, i, src, dst):
        cp = pltpu.make_async_copy(src, dst, wsem.at[i])
        cp.start()
        loads[name] = cp

    load("sg", 0, sg_ref, sgt)
    load("su", 1, su_ref, sut)
    load("wg", 2, wg_ref, wga.at[:, 0:FR])
    load("wu", 3, wu_ref, wua.at[:, 0:FR])
    load("lg0", 4, lg_ref, lga.at[0:RANK])
    load("lg1", 5, lg_ref, lga.at[RANK : 2 * RANK])
    load("lu0", 6, lu_ref, lua.at[0:RANK])
    load("lu1", 7, lu_ref, lua.at[RANK : 2 * RANK])
    load("wd", 8, wd_ref, wda.at[0:FR])
    load("ld0", 9, ld_ref, wda.at[FR : FR + RANK])
    load("ld1", 10, ld_ref, wda.at[FR + RANK : FR + 2 * RANK])
    load("sd", 11, sd_ref, sdt)

    for a, ref in enumerate((x_ref, dy_ref)):
        v = ref[...].astype(F32)
        g[a, r] = jnp.concatenate([v[:, : DC // 2], v[:, DC // 2 :]], axis=0).astype(BF16)

    pl.semaphore_wait(barrier, len(peers))

    started = []
    sems = {}

    def rsem(key):
        if key not in sems:
            sems[key] = len(sems)
        return rs.at[sems[key]]

    def send(src, dst, key, **to):
        cp = pltpu.make_async_remote_copy(
            src_ref=src, dst_ref=dst, send_sem=ss.at[len(started)], recv_sem=rsem(key),
            device_id=dev(**to), device_id_type=MESH,
        )
        cp.start()
        started.append(cp)

    def arrived(dst, key):
        pltpu.make_async_remote_copy(
            src_ref=dst, dst_ref=dst, send_sem=ss.at[0], recv_sem=rsem(key),
            device_id=dev(dk=1), device_id_type=MESH,
        ).wait_recv()

    def block(a, dy, dz):
        return g.at[a, ((y + dy) % NY) * NZ + (z + dz) % NZ]

    def gather_z(a):
        for dz in ZORD:
            send(block(a, 0, 0), block(a, 0, 0), ("gz", a, dz), dz=dz)

    def gather_y(a):
        for dz in (0,) + ZORD:
            b = block(a, 0, -dz)
            if dz:
                arrived(b, ("gz", a, dz))
            for dy in (1, 3):
                send(b, b, ("gy", a, dy, dz), dy=dy)

    def gather_forward(a, dzs):
        for dz in dzs:
            for dy, cols in ((1, slice(0, DC // 4)), (3, slice(DC // 4, DC // 2))):
                b = block(a, -dy, -dz)
                arrived(b, ("gy", a, dy, dz))
                send(b.at[:, cols], b.at[:, cols], ("gf", a, dy, dz), dy=dy)

    def gather_end(a):
        for dz in (0,) + ZORD:
            b = block(a, 2, -dz)
            arrived(b.at[:, 0 : DC // 4], ("gf", a, 1, dz))
            arrived(b.at[:, DC // 4 : DC // 2], ("gf", a, 3, dz))
        for i in range(8):
            v = g[a, 4 * i : 4 * i + 4].astype(F32).reshape(4, 2, 8, DC // 2)
            rows = slice(32 * i, 32 * i + 32)
            pan[a, rows, 0 : DC // 2] = v[:, 0].reshape(32, DC // 2).astype(BF16)
            pan[a, rows, DC // 2 : DC] = v[:, 1].reshape(32, DC // 2).astype(BF16)

    gather_z(0)
    gather_z(1)

    rows16 = lax.broadcasted_iota(jnp.int32, (RANK, 128), 0)
    lanes = lax.broadcasted_iota(jnp.int32, (RANK, 128), 1)
    twice = ((lanes % RANK == rows16) & (lanes < 2 * RANK)).astype(F32).astype(BF16)
    for name, src, dst in (("sg", sgt, wga), ("su", sut, wua)):
        loads[name].wait()
        dst[:, FR:FA] = nn(src[...], twice).astype(BF16)
    for dst in (lga, lua):
        dst[2 * RANK : 128] = jnp.zeros((128 - 2 * RANK, FR), BF16)
    wda[FR + 2 * RANK : FA] = jnp.zeros((FA - FR - 2 * RANK, DC), BF16)

    gather_y(0)
    loads["sd"].wait()
    sda[...] = nn(sdt[...], twice).astype(BF16)
    gather_forward(0, (0,) + ZORD)
    gather_y(1)
    for name in ("wg", "wu", "lg0", "lg1", "lu0", "lu1"):
        loads[name].wait()
    gather_end(0)

    other = pl.multiple_of((1 - k) * HALF, HALF)
    mine = pl.multiple_of(k * HALF, HALF)
    myrow = pl.multiple_of(k * HALF + x * QUART, QUART)

    def sum_cores(a):
        send(part.at[a, pl.ds(other, HALF)], sib.at[a], ("sib", a), dk=1)

    def sum_x(a):
        arrived(sib.at[a], ("sib", a))
        for q in range(NX):
            rows = pl.ds(pl.multiple_of(mine + q * QUART, QUART), QUART)
            v = part[a, rows, :] + sib[a, q * QUART : (q + 1) * QUART, :]
            own[a, q] = v
            xs[a, q] = v.astype(BF16)
        for dx in (1, 3, 2):
            send(xs.at[a, (x + dx) % NX], xr.at[a, dx - 1], ("xr", a, dx), dx=dx)

    def total_x(a):
        for dx in (1, 3, 2):
            arrived(xr.at[a, dx - 1], ("xr", a, dx))
        return own[a, x] + xr[a, 0].astype(F32) + xr[a, 1].astype(F32) + xr[a, 2].astype(F32)

    def forward_part(a, w, lift):
        o = nn(pan[0], w[:, 768:FA])
        sel = split_inner(o[:, 128:256])
        part[a, :, 768:FR] = o[:, 0:128] + nn(sel, lift[:, 768:FR])
        for j in range(3):
            cols = slice(256 * j, 256 * (j + 1))
            part[a, :, cols] = nn(pan[0], w[:, cols]) + nn(sel, lift[:, cols])

    forward_part(0, wga, lga)
    sum_cores(0)
    forward_part(1, wua, lua)
    sum_cores(1)
    sum_x(0)
    sum_x(1)
    gather_forward(1, (0,) + ZORD)

    def spread(a):
        b = act.at[a, pl.ds(myrow, QUART), 0:FR]
        for dx in (1, 3, 2):
            send(b, b, ("ax", a, dx), dx=dx)
        send(b, b, ("ak", a, 0), dk=1)

    def spread_on(a):
        for dx in (1, 3, 2):
            rows = pl.multiple_of(k * HALF + ((x - dx) % NX) * QUART, QUART)
            b = act.at[a, pl.ds(rows, QUART), 0:FR]
            arrived(b, ("ax", a, dx))
            send(b, b, ("ak", a, dx), dk=1)

    def spread_end(a):
        for dx in (0, 1, 3, 2):
            rows = pl.multiple_of((1 - k) * HALF + ((x - dx) % NX) * QUART, QUART)
            arrived(act.at[a, pl.ds(rows, QUART), 0:FR], ("ak", a, dx))

    gate = total_x(0)
    up = total_x(1)
    sigmoid = jax.nn.sigmoid(gate)
    act[0, pl.ds(myrow, QUART), 0:FR] = (gate * sigmoid * up).astype(BF16)
    spread(0)
    own[0, x] = gate
    own[1, x] = up

    for name in ("wd", "ld0", "ld1"):
        loads[name].wait()
    gather_end(1)
    spread_on(0)
    o = nt(pan[1], wda[768:FA, :])
    sel = split_inner(o[:, 128:256])
    part[2, :, 768:FR] = o[:, 0:128] + nt(sel, sda[768:FR, :])
    for j in range(3):
        cols = slice(256 * j, 256 * (j + 1))
        part[2, :, cols] = nt(pan[1], wda[cols, :]) + nt(sel, sda[cols, :])
    sum_cores(2)

    def y_send(a, j, value):
        cols = slice(CW * j, CW * (j + 1))
        mf[a, :, cols] = value
        ms[a, :, cols] = value.astype(BF16)
        for dy in YORD:
            rows = pl.multiple_of(((y + dy) % NY) * TY, TY)
            send(ms.at[a, pl.ds(rows, TY), cols], ry.at[a, dy - 1, :, cols], ("ry", a, j, dy), dy=dy)

    def z_send(a, j):
        cols = slice(CW * j, CW * (j + 1))
        for dy in YORD:
            arrived(ry.at[a, dy - 1, :, cols], ("ry", a, j, dy))
        v = mf[a, pl.ds(pl.multiple_of(y * TY, TY), TY), cols]
        for dy in YORD:
            v = v + ry[a, dy - 1, :, cols].astype(F32)
        zo[a, :, cols] = v
        if j % 2 == 0:
            return
        first = zo[a, :, CW * (j - 1) : CW * j].reshape(NZ, 8, CW)
        zs[a, j // 2] = jnp.concatenate([first, v.reshape(NZ, 8, CW)], axis=1).astype(BF16)
        for dz in ZORD:
            send(zs.at[a, j // 2, (z + dz) % NZ], zr.at[a, j // 2, dz - 1], ("zr", a, j // 2, dz), dz=dz)

    def z_end(a, out_ref):
        for h in range(NCH // 2):
            v = zo[a, pl.ds(pl.multiple_of(z * 8, 8), 8), 2 * CW * h : 2 * CW * (h + 1)]
            v = jnp.concatenate([v[:, :CW], v[:, CW:]], axis=0)
            for dz in ZORD:
                arrived(zr.at[a, h, dz - 1], ("zr", a, h, dz))
            for dz in ZORD:
                v = v + zr[a, h, dz - 1].astype(F32)
            out_ref[:, 2 * CW * h : 2 * CW * h + CW] = v[0:8].astype(BF16)
            out_ref[:, 2 * CW * h + CW : 2 * CW * (h + 1)] = v[8:16].astype(BF16)

    def down(j):
        y_send(0, j, nn(act[0], wda[:, CW * j : CW * (j + 1)]))

    def back(j):
        rows = slice(CW * j, CW * (j + 1))
        y_send(1, j, nt(act[1], wga[rows, :]) + nt(act[2], wua[rows, :]))

    spread_end(0)
    act[0, :, FR:FA] = split_inner(nn(act[0, :, 0:FR], sda[...]))
    down(0)
    sum_x(2)
    down(1)
    down(2)
    down(3)

    hidden_gradient = total_x(2)
    gate = own[0, x]
    up = own[1, x]
    sigmoid = jax.nn.sigmoid(gate)
    act[1, pl.ds(myrow, QUART), 0:FR] = (
        hidden_gradient * up * sigmoid * (1.0 + gate * (1.0 - sigmoid))
    ).astype(BF16)
    act[2, pl.ds(myrow, QUART), 0:FR] = (hidden_gradient * gate * sigmoid).astype(BF16)
    spread(1)
    spread(2)
    z_send(0, 0)
    spread_on(1)
    spread_on(2)
    z_send(0, 1)
    spread_end(1)
    act[1, :, FR:FA] = split_inner(nt(act[1, :, 0:FR], lga[...]))
    spread_end(2)
    act[2, :, FR:FA] = split_inner(nt(act[2, :, 0:FR], lua[...]))
    back(0)
    z_send(0, 2)
    back(1)
    z_send(0, 3)
    back(2)
    back(3)
    z_send(1, 0)
    z_send(1, 1)
    z_end(0, mixed_ref)
    z_send(1, 2)
    z_send(1, 3)
    z_end(1, tg_ref)
    for cp in started:
        cp.wait_send()


def on_device(tokens, gate_w, up_w, down_w, gate_s, gate_l, up_s, up_l, down_s, down_l, cotangent):
    vmem = pl.BlockSpec(memory_space=pltpu.VMEM)
    anywhere = pl.BlockSpec(memory_space=pl.ANY)
    out = jax.ShapeDtypeStruct((T // NY // NZ, DC), BF16)
    return pl.pallas_call(
        kernel,
        out_shape=(out, out),
        in_specs=[vmem] * 2 + [anywhere] * 9,
        out_specs=(vmem, vmem),
        scratch_shapes=[
            pltpu.VMEM((DC, FA), BF16),
            pltpu.VMEM((DC, FA), BF16),
            pltpu.VMEM((FA, DC), BF16),
            pltpu.VMEM((128, FR), BF16),
            pltpu.VMEM((128, FR), BF16),
            pltpu.VMEM((FR, 128), BF16),
            pltpu.VMEM((DC, RANK), BF16),
            pltpu.VMEM((DC, RANK), BF16),
            pltpu.VMEM((FR, RANK), BF16),
            pltpu.VMEM((2, NY * NZ, 16, DC // 2), BF16),
            pltpu.VMEM((2, T, DC), BF16),
            pltpu.VMEM((3, T, FR), F32),
            pltpu.VMEM((3, HALF, FR), F32),
            pltpu.VMEM((3, NX, QUART, FR), F32),
            pltpu.VMEM((3, NX, QUART, FR), BF16),
            pltpu.VMEM((3, NX - 1, QUART, FR), BF16),
            pltpu.VMEM((3, T, FA), BF16),
            pltpu.VMEM((2, T, DC), F32),
            pltpu.VMEM((2, T, DC), BF16),
            pltpu.VMEM((2, NY - 1, TY, DC), BF16),
            pltpu.VMEM((2, TY, DC), F32),
            pltpu.VMEM((2, NCH // 2, NZ, 16, CW), BF16),
            pltpu.VMEM((2, NCH // 2, NZ - 1, 16, CW), BF16),
            pltpu.SemaphoreType.DMA((12,)),
            pltpu.SemaphoreType.DMA((200,)),
            pltpu.SemaphoreType.DMA((200,)),
        ],
        compiler_params=pltpu.CompilerParams(
            collective_id=0, has_side_effects=True, vmem_limit_bytes=58 * 2**20
        ),
        name="lora_swiglu",
    )(tokens, cotangent, gate_w, up_w, down_w, gate_s, gate_l, up_s, up_l, down_s, down_l)


def solution(mesh):
    placed = (
        P("row", "col"),
        P("col", "row"),
        P("col", "row"),
        P("row", "col"),
        P("col", None),
        P(None, "row"),
        P("col", None),
        P(None, "row"),
        P("row", None),
        P(None, "col"),
        P("row", "col"),
    )
    return jax.shard_map(
        on_device,
        mesh=mesh,
        in_specs=placed,
        out_specs=(P("row", "col"), P("row", "col")),
        check_vma=False,
    )
```

```python
import jax
import jax.numpy as jnp
from jax import lax
from jax.experimental import pallas as pl
from jax.experimental.pallas import tpu as pltpu
from jax.sharding import PartitionSpec as P

MESH = pl.DeviceIdType.MESH
F32, BF16 = jnp.float32, jnp.bfloat16

NX, NCORE, NY, NZ = 4, 2, 4, 8
T, DC, FR, RANK = 256, 2048, 896, 16
FA = 1024
HALF, QUART = T // NCORE, T // NCORE // NX
TY = T // NY
CW = 512
NCH = DC // CW
ZGROUPS = ((0,), (1, 7), (2, 6), (3, 5, 4))
SCALE = 0.5


def nn(a, b):
    return jnp.dot(a, b, preferred_element_type=F32)


def nt(a, b):
    return lax.dot_general(a, b, (((1,), (1,)), ((), ())), preferred_element_type=F32)


def tn(a, b):
    return lax.dot_general(a, b, (((0,), (0,)), ((), ())), preferred_element_type=F32)


def split_inner(inner):
    top = inner.astype(BF16).astype(F32)
    lane = lax.broadcasted_iota(jnp.int32, inner.shape, 1)
    return (jnp.where(lane < RANK, top, inner - top) * SCALE).astype(BF16)


def kernel(
    x_ref, dy_ref, wg_ref, wu_ref, wd_ref, sg_ref, lg_ref, su_ref, lu_ref, sd_ref, ld_ref,
    mixed_ref, tg_ref,
    xin, wga, wua, wda, lga, lua, sda, sgt, sut, sdt,
    g, pan, acc, part, sib, own, xs, xr, act, mf, ms, ry, rp, zo, zs, zr,
    wsem, ss, rs,
):
    r, c = lax.axis_index("row"), lax.axis_index("col")
    y, z = r // NZ, r % NZ
    x, k = c // NCORE, c % NCORE

    def dev(dx=0, dk=0, dy=0, dz=0):
        return {
            "row": ((y + dy) % NY) * NZ + (z + dz) % NZ,
            "col": ((x + dx) % NX) * NCORE + (k + dk) % NCORE,
        }

    peers = (
        [dict(dz=d) for d in range(1, NZ)]
        + [dict(dy=d) for d in range(1, NY)]
        + [dict(dx=d) for d in range(1, NX)]
        + [dict(dk=1)]
    )
    barrier = pltpu.get_barrier_semaphore()
    for p in peers:
        pl.semaphore_signal(barrier, inc=1, device_id=dev(**p), device_id_type=MESH)

    loads = {}

    def load(name, i, src, dst):
        cp = pltpu.make_async_copy(src, dst, wsem.at[i])
        cp.start()
        loads[name] = cp

    load("x", 12, x_ref, xin.at[0])
    load("dy", 13, dy_ref, xin.at[1])
    loads["x"].wait()
    loads["dy"].wait()

    for a in range(2):
        v = xin[a].astype(F32)
        for h in range(2):
            q = DC // 4
            g[a, h, r] = jnp.concatenate(
                [v[:, 2 * h * q : (2 * h + 1) * q], v[:, (2 * h + 1) * q : (2 * h + 2) * q]], axis=0
            ).astype(BF16)

    pl.semaphore_wait(barrier, len(peers))

    recv_sems, send_sems = {}, {}

    def sem_of(ref, table, key):
        return ref.at[table.setdefault(key, len(table))]

    def send(src, dst, sent, key, **to):
        cp = pltpu.make_async_remote_copy(
            src_ref=src, dst_ref=dst, send_sem=sem_of(ss, send_sems, sent), recv_sem=sem_of(rs, recv_sems, key),
            device_id=dev(**to), device_id_type=MESH,
        )
        cp.start()

    def arrived(like, key):
        pltpu.make_async_remote_copy(
            src_ref=like, dst_ref=like, send_sem=ss.at[0], recv_sem=sem_of(rs, recv_sems, key),
            device_id=dev(dk=1), device_id_type=MESH,
        ).wait_recv()

    def all_sent(like, sent):
        pltpu.make_async_remote_copy(
            src_ref=like, dst_ref=like, send_sem=sem_of(ss, send_sems, sent), recv_sem=rs.at[0],
            device_id=dev(dk=1), device_id_type=MESH,
        ).wait_send()

    def block(a, h, dy, dz):
        return g.at[a, h, ((y + dy) % NY) * NZ + (z + dz) % NZ]

    def gather_z(a, h):
        b = block(a, h, 0, 0)
        for i, group in enumerate(ZGROUPS[1:]):
            for dz in group:
                send(b, b, ("g", a, h), ("gz", a, h, i + 1), dz=dz)

    def gather_y(a, h):
        for i, group in enumerate(ZGROUPS):
            if i:
                arrived(g.at[a, h, 0 : len(group)], ("gz", a, h, i))
            for dz in group:
                b = block(a, h, 0, -dz)
                send(b, b, ("g", a, h), ("gy", a, h, i), dy=(1, 3)[h])
                send(b, b, ("g", a, h), ("ge", a, h), dy=(3, 1)[h])

    def gather_forward(a, h):
        dy = (1, 3)[h]
        for i, group in enumerate(ZGROUPS):
            arrived(g.at[a, h, 0 : len(group)], ("gy", a, h, i))
            for dz in group:
                b = block(a, h, -dy, -dz)
                send(b, b, ("g", a, h), ("gf", a, h), dy=dy)

    def gather_end(a, h):
        arrived(g.at[a, h, 0:NZ], ("ge", a, h))
        arrived(g.at[a, h, 0:NZ], ("gf", a, h))
        for i in range(4):
            v = g[a, h, 8 * i : 8 * i + 8].astype(F32).reshape(8, 2, 8, DC // 4)
            rows = slice(64 * i, 64 * i + 64)
            pan[a, h, rows, 0 : DC // 4] = v[:, 0].reshape(64, DC // 4).astype(BF16)
            pan[a, h, rows, DC // 4 : DC // 2] = v[:, 1].reshape(64, DC // 4).astype(BF16)

    gather_z(0, 0)
    gather_z(0, 1)
    load("sg", 0, sg_ref, sgt)
    load("su", 1, su_ref, sut)
    load("wg", 2, wg_ref, wga.at[:, 0:FR])
    load("wu", 3, wu_ref, wua.at[:, 0:FR])
    load("lg0", 4, lg_ref, lga.at[0:RANK])
    load("lg1", 5, lg_ref, lga.at[RANK : 2 * RANK])
    load("lu0", 6, lu_ref, lua.at[0:RANK])
    load("lu1", 7, lu_ref, lua.at[RANK : 2 * RANK])
    load("wd", 8, wd_ref, wda.at[0:FR])
    load("ld0", 9, ld_ref, wda.at[FR : FR + RANK])
    load("ld1", 10, ld_ref, wda.at[FR + RANK : FR + 2 * RANK])
    load("sd", 11, sd_ref, sdt)

    rows16 = lax.broadcasted_iota(jnp.int32, (RANK, 128), 0)
    lanes = lax.broadcasted_iota(jnp.int32, (RANK, 128), 1)
    twice = ((lanes % RANK == rows16) & (lanes < 2 * RANK)).astype(F32).astype(BF16)
    for name, src, dst in (("sg", sgt, wga), ("su", sut, wua)):
        loads[name].wait()
        dst[:, FR:FA] = tn(src[...], twice).astype(BF16)
    for dst in (lga, lua):
        dst[2 * RANK : 128] = jnp.zeros((128 - 2 * RANK, FR), BF16)
    wda[FR + 2 * RANK : FA] = jnp.zeros((FA - FR - 2 * RANK, DC), BF16)

    gather_y(0, 0)
    gather_y(0, 1)
    gather_z(1, 0)
    gather_z(1, 1)
    gather_forward(0, 0)
    gather_forward(0, 1)
    loads["sd"].wait()
    sda[...] = tn(sdt[...], twice).astype(BF16)
    gather_y(1, 0)
    gather_y(1, 1)
    for name in ("wg", "wu", "lg0", "lg1", "lu0", "lu1"):
        loads[name].wait()

    other = pl.multiple_of((1 - k) * HALF, HALF)
    mine = pl.multiple_of(k * HALF, HALF)
    myrow = pl.multiple_of(k * HALF + x * QUART, QUART)

    def sum_cores(a):
        send(part.at[a, pl.ds(other, HALF)], sib.at[a], "sib", ("sib", a), dk=1)

    def sum_x(a):
        arrived(sib.at[a], ("sib", a))
        for q in range(NX):
            rows = pl.ds(pl.multiple_of(mine + q * QUART, QUART), QUART)
            v = part[a, rows, :] + sib[a, q * QUART : (q + 1) * QUART, :]
            own[a, q] = v
            xs[a, q] = v.astype(BF16)
        for dx in (1, 3, 2):
            send(xs.at[a, (x + dx) % NX], xr.at[a, dx - 1], "xr", ("xr", a), dx=dx)

    def total_x(a):
        arrived(xr.at[a], ("xr", a))
        return own[a, x] + xr[a, 0].astype(F32) + xr[a, 1].astype(F32) + xr[a, 2].astype(F32)

    low, high = slice(0, DC // 2), slice(DC // 2, DC)
    tiles = [slice(256 * j, 256 * (j + 1)) for j in range(4)]

    def forward_low(a, w):
        for t in tiles:
            acc[a, :, t] = nn(pan[0, 0], w[low, t])

    def forward_high(a, w, lift):
        o = acc[a, :, tiles[3]] + nn(pan[0, 1], w[high, tiles[3]])
        sel = split_inner(o[:, 128:256])
        part[a, :, 768:FR] = o[:, 0:128] + nn(sel, lift[:, 768:FR])
        for t in tiles[:3]:
            part[a, :, t] = acc[a, :, t] + nn(pan[0, 1], w[high, t]) + nn(sel, lift[:, t])

    gather_end(0, 0)
    forward_low(0, wga)
    forward_low(1, wua)
    gather_end(0, 1)
    forward_high(0, wga, lga)
    sum_cores(0)
    forward_high(1, wua, lua)
    sum_cores(1)
    gather_forward(1, 0)
    sum_x(0)
    gather_forward(1, 1)
    sum_x(1)

    for name in ("wd", "ld0", "ld1"):
        loads[name].wait()
    gather_end(1, 0)
    for t in tiles:
        acc[0, :, t] = nt(pan[1, 0], wda[t, low])
    gather_end(1, 1)
    o = acc[0, :, tiles[3]] + nt(pan[1, 1], wda[tiles[3], high])
    sel = split_inner(o[:, 128:256])
    part[2, :, 768:FR] = o[:, 0:128] + nt(sel, sda[768:FR, :])
    for t in tiles[:3]:
        part[2, :, t] = acc[0, :, t] + nt(pan[1, 1], wda[t, high]) + nt(sel, sda[t, :])
    sum_cores(2)

    def spread(a):
        b = act.at[a, pl.ds(myrow, QUART), 0:FR]
        for dx in (1, 3, 2):
            send(b, b, ("a", a), ("ax", a), dx=dx)
        send(b, b, ("a", a), ("ak", a), dk=1)

    def spread_on(a):
        arrived(act.at[a, 0 : 3 * QUART, 0:FR], ("ax", a))
        for dx in (1, 3, 2):
            rows = pl.multiple_of(k * HALF + ((x - dx) % NX) * QUART, QUART)
            b = act.at[a, pl.ds(rows, QUART), 0:FR]
            send(b, b, ("a", a), ("ak", a), dk=1)

    def spread_end(a):
        arrived(act.at[a, 0:HALF, 0:FR], ("ak", a))

    gate = total_x(0)
    up = total_x(1)
    sigmoid = jax.nn.sigmoid(gate)
    act[0, pl.ds(myrow, QUART), 0:FR] = (gate * sigmoid * up).astype(BF16)
    spread(0)

    def at_y(d):
        return pl.ds(pl.multiple_of(((y + d) % NY) * TY, TY), TY)

    def parts_of(j):
        return slice(CW * j, CW * j + CW // 2), slice(CW * j + CW // 2, CW * (j + 1))

    def y_send(a, j, value):
        first, rest = parts_of(j)
        cols = slice(CW * j, CW * (j + 1))
        mf[a, :, cols] = value
        ms[a, :, cols] = value.astype(BF16)
        send(ms.at[a, at_y(2), first], rp.at[a, j, 0], ("y", a), ("rp", a, j), dy=1)
        send(ms.at[a, at_y(2), rest], rp.at[a, j, 1], ("y", a), ("rp", a, j), dy=3)
        send(ms.at[a, at_y(1), rest], ry.at[a, 0, :, rest], ("y", a), ("ry", a, j), dy=1)
        send(ms.at[a, at_y(3), first], ry.at[a, 1, :, first], ("y", a), ("ry", a, j), dy=3)

    def y_relay(a, j):
        first, rest = parts_of(j)
        arrived(rp.at[a, j], ("rp", a, j))
        for i, (dy, cols) in enumerate(((1, first), (3, rest))):
            ms[a, at_y(dy), cols] = (mf[a, at_y(dy), cols] + rp[a, j, i].astype(F32)).astype(BF16)
            send(ms.at[a, at_y(dy), cols], ry.at[a, i, :, cols], ("y", a), ("ry", a, j), dy=dy)

    def z_send(a, j):
        cols = slice(CW * j, CW * (j + 1))
        arrived(ry.at[a, :, :, cols], ("ry", a, j))
        v = mf[a, at_y(0), cols] + ry[a, 0, :, cols].astype(F32) + ry[a, 1, :, cols].astype(F32)
        v = v.reshape(NZ, 8, CW)
        v = jnp.concatenate([v[:, :, : CW // 2], v[:, :, CW // 2 :]], axis=1)
        zo[a, j] = v
        zs[a, j] = v.astype(BF16)
        for dz in (4, 3, 5, 2, 6, 1, 7):
            send(zs.at[a, j, (z + dz) % NZ], zr.at[a, j, dz - 1], ("z", a), ("zr", a, j), dz=dz)

    def z_end(a, j, out_ref):
        v = zo[a, j, z]
        arrived(zr.at[a, j], ("zr", a, j))
        for dz in range(1, NZ):
            v = v + zr[a, j, dz - 1].astype(F32)
        first, rest = parts_of(j)
        out_ref[:, first] = v[0:8].astype(BF16)
        out_ref[:, rest] = v[8:16].astype(BF16)

    def down(j):
        y_send(0, j, nn(act[0], wda[:, CW * j : CW * (j + 1)]))

    def back(j):
        rows = slice(CW * j, CW * (j + 1))
        y_send(1, j, nt(act[1], wga[rows, :]) + nt(act[2], wua[rows, :]))

    sum_x(2)
    spread_on(0)
    spread_end(0)
    act[0, :, FR:FA] = split_inner(nn(act[0, :, 0:FR], sda[...]))
    down(0)
    down(1)

    hidden_gradient = total_x(2)
    act[1, pl.ds(myrow, QUART), 0:FR] = (
        hidden_gradient * up * sigmoid * (1.0 + gate * (1.0 - sigmoid))
    ).astype(BF16)
    act[2, pl.ds(myrow, QUART), 0:FR] = (hidden_gradient * gate * sigmoid).astype(BF16)
    spread(1)
    spread(2)

    y_relay(0, 0)
    down(2)
    y_relay(0, 1)
    down(3)
    y_relay(0, 2)
    spread_on(1)
    z_send(0, 0)
    y_relay(0, 3)
    spread_on(2)
    z_send(0, 1)
    spread_end(1)
    act[1, :, FR:FA] = split_inner(nt(act[1, :, 0:FR], lga[...]))
    spread_end(2)
    act[2, :, FR:FA] = split_inner(nt(act[2, :, 0:FR], lua[...]))
    back(0)
    z_send(0, 2)
    back(1)
    y_relay(1, 0)
    z_send(0, 3)
    back(2)
    y_relay(1, 1)
    back(3)
    y_relay(1, 2)
    z_send(1, 0)
    y_relay(1, 3)
    z_send(1, 1)
    for j in range(NCH):
        z_end(0, j, mixed_ref)
    z_send(1, 2)
    z_send(1, 3)
    for j in range(NCH):
        z_end(1, j, tg_ref)
    for a in range(2):
        for h in range(2):
            all_sent(g.at[a, h, 0:31], ("g", a, h))
    all_sent(sib, "sib")
    all_sent(xr, "xr")
    for a in range(3):
        all_sent(act.at[a, 0 : 7 * QUART, 0:FR], ("a", a))
    for a in range(2):
        all_sent(ms.at[a, 0 : 3 * TY], ("y", a))
        all_sent(zr.at[a], ("z", a))


def on_device(tokens, gate_w, up_w, down_w, gate_s, gate_l, up_s, up_l, down_s, down_l, cotangent):
    vmem = pl.BlockSpec(memory_space=pltpu.VMEM)
    anywhere = pl.BlockSpec(memory_space=pl.ANY)
    out = jax.ShapeDtypeStruct((T // NY // NZ, DC), BF16)
    return pl.pallas_call(
        kernel,
        out_shape=(out, out),
        in_specs=[anywhere] * 11,
        out_specs=(vmem, vmem),
        scratch_shapes=[
            pltpu.VMEM((2, T // NY // NZ, DC), BF16),
            pltpu.VMEM((DC, FA), BF16),
            pltpu.VMEM((DC, FA), BF16),
            pltpu.VMEM((FA, DC), BF16),
            pltpu.VMEM((128, FR), BF16),
            pltpu.VMEM((128, FR), BF16),
            pltpu.VMEM((FR, 128), BF16),
            pltpu.VMEM((RANK, DC), BF16),
            pltpu.VMEM((RANK, DC), BF16),
            pltpu.VMEM((RANK, FR), BF16),
            pltpu.VMEM((2, 2, NY * NZ, 16, DC // 4), BF16),
            pltpu.VMEM((2, 2, T, DC // 2), BF16),
            pltpu.VMEM((2, T, FA), F32),
            pltpu.VMEM((3, T, FR), F32),
            pltpu.VMEM((3, HALF, FR), F32),
            pltpu.VMEM((3, NX, QUART, FR), F32),
            pltpu.VMEM((3, NX, QUART, FR), BF16),
            pltpu.VMEM((3, NX - 1, QUART, FR), BF16),
            pltpu.VMEM((3, T, FA), BF16),
            pltpu.VMEM((2, T, DC), F32),
            pltpu.VMEM((2, T, DC), BF16),
            pltpu.VMEM((2, 2, TY, DC), BF16),
            pltpu.VMEM((2, NCH, 2, TY, CW // 2), BF16),
            pltpu.VMEM((2, NCH, NZ, 16, CW // 2), F32),
            pltpu.VMEM((2, NCH, NZ, 16, CW // 2), BF16),
            pltpu.VMEM((2, NCH, NZ - 1, 16, CW // 2), BF16),
            pltpu.SemaphoreType.DMA((14,)),
            pltpu.SemaphoreType.DMA((13,)),
            pltpu.SemaphoreType.DMA((72,)),
        ],
        compiler_params=pltpu.CompilerParams(
            collective_id=0, has_side_effects=True, vmem_limit_bytes=58 * 2**20
        ),
        name="lora_swiglu",
    )(tokens, cotangent, gate_w, up_w, down_w, gate_s.T, gate_l, up_s.T, up_l, down_s.T, down_l)


def solution(mesh):
    placed = (
        P("row", "col"),
        P("col", "row"),
        P("col", "row"),
        P("row", "col"),
        P("col", None),
        P(None, "row"),
        P("col", None),
        P(None, "row"),
        P("row", None),
        P(None, "col"),
        P("row", "col"),
    )
    return jax.shard_map(
        on_device,
        mesh=mesh,
        in_specs=placed,
        out_specs=(P("row", "col"), P("row", "col")),
        check_vma=False,
    )
```

```python
import jax
import jax.numpy as jnp
from jax import lax
from jax.experimental import pallas as pl
from jax.experimental.pallas import tpu as pltpu
from jax.sharding import PartitionSpec as P

MESH = pl.DeviceIdType.MESH
F32, BF16 = jnp.float32, jnp.bfloat16

NX, NCORE, NY, NZ = 4, 2, 4, 8
T, DC, FR, RANK = 256, 2048, 896, 16
FA = 1024
HALF, QUART = T // NCORE, T // NCORE // NX
TY = T // NY
CW = 512
NCH = DC // CW
ZGROUPS = ((0,), (1, 7), (2, 6), (3, 5, 4))
SCALE = 0.5
RS_DIRECT = ((1, 2), (1, 3))


def nn(a, b):
    return jnp.dot(a, b, preferred_element_type=F32)


def nt(a, b):
    return lax.dot_general(a, b, (((1,), (1,)), ((), ())), preferred_element_type=F32)


def tn(a, b):
    return lax.dot_general(a, b, (((0,), (0,)), ((), ())), preferred_element_type=F32)


def split_inner(inner):
    top = inner.astype(BF16).astype(F32)
    lane = lax.broadcasted_iota(jnp.int32, inner.shape, 1)
    return (jnp.where(lane < RANK, top, inner - top) * SCALE).astype(BF16)


def kernel(
    x_ref, dy_ref, wg_ref, wu_ref, wd_ref, sg_ref, lg_ref, su_ref, lu_ref, sd_ref, ld_ref,
    mixed_ref, tg_ref,
    xin, wga, wua, wda, lga, lua, sda, sgt, sut, sdt,
    g, pan, acc, part, sib, own, xs, xr, act, mf, ms, ry, rp, zo, zs, zr,
    wsem, ss, rs,
):
    r, c = lax.axis_index("row"), lax.axis_index("col")
    y, z = r // NZ, r % NZ
    x, k = c // NCORE, c % NCORE

    def dev(dx=0, dk=0, dy=0, dz=0):
        return {
            "row": ((y + dy) % NY) * NZ + (z + dz) % NZ,
            "col": ((x + dx) % NX) * NCORE + (k + dk) % NCORE,
        }

    peers = (
        [dict(dz=d) for d in range(1, NZ)]
        + [dict(dy=d) for d in range(1, NY)]
        + [dict(dx=d) for d in range(1, NX)]
        + [dict(dk=1)]
    )
    barrier = pltpu.get_barrier_semaphore()
    for p in peers:
        pl.semaphore_signal(barrier, inc=1, device_id=dev(**p), device_id_type=MESH)

    loads = {}

    def load(name, i, src, dst):
        cp = pltpu.make_async_copy(src, dst, wsem.at[i])
        cp.start()
        loads[name] = cp

    load("x", 12, x_ref, xin.at[0])
    load("dy", 13, dy_ref, xin.at[1])
    loads["x"].wait()
    loads["dy"].wait()

    for a in range(2):
        v = xin[a].astype(F32)
        for h in range(2):
            q = DC // 4
            g[a, h, r] = jnp.concatenate(
                [v[:, 2 * h * q : (2 * h + 1) * q], v[:, (2 * h + 1) * q : (2 * h + 2) * q]], axis=0
            ).astype(BF16)

    pl.semaphore_wait(barrier, len(peers))

    recv_sems, send_sems = {}, {}

    def sem_of(ref, table, key):
        return ref.at[table.setdefault(key, len(table))]

    def send(src, dst, sent, key, **to):
        cp = pltpu.make_async_remote_copy(
            src_ref=src, dst_ref=dst, send_sem=sem_of(ss, send_sems, sent), recv_sem=sem_of(rs, recv_sems, key),
            device_id=dev(**to), device_id_type=MESH,
        )
        cp.start()

    def arrived(like, key):
        pltpu.make_async_remote_copy(
            src_ref=like, dst_ref=like, send_sem=ss.at[0], recv_sem=sem_of(rs, recv_sems, key),
            device_id=dev(dk=1), device_id_type=MESH,
        ).wait_recv()

    def all_sent(like, sent):
        pltpu.make_async_remote_copy(
            src_ref=like, dst_ref=like, send_sem=sem_of(ss, send_sems, sent), recv_sem=rs.at[0],
            device_id=dev(dk=1), device_id_type=MESH,
        ).wait_send()

    def block(a, h, dy, dz):
        return g.at[a, h, ((y + dy) % NY) * NZ + (z + dz) % NZ]

    def gather_z(a, h):
        b = block(a, h, 0, 0)
        for i, group in enumerate(ZGROUPS[1:]):
            for dz in group:
                send(b, b, ("g", a, h), ("gz", a, h, i + 1), dz=dz)

    def gather_y(a, h):
        for i, group in enumerate(ZGROUPS):
            if i:
                arrived(g.at[a, h, 0 : len(group)], ("gz", a, h, i))
            for dz in group:
                b = block(a, h, 0, -dz)
                send(b, b, ("g", a, h), ("gy", a, h, i), dy=(1, 3)[h])
                send(b, b, ("g", a, h), ("ge", a, h), dy=(3, 1)[h])

    def gather_forward(a, h):
        dy = (1, 3)[h]
        for i, group in enumerate(ZGROUPS):
            arrived(g.at[a, h, 0 : len(group)], ("gy", a, h, i))
            for dz in group:
                b = block(a, h, -dy, -dz)
                send(b, b, ("g", a, h), ("gf", a, h), dy=dy)

    def gather_end(a, h):
        arrived(g.at[a, h, 0:NZ], ("ge", a, h))
        arrived(g.at[a, h, 0:NZ], ("gf", a, h))
        for i in range(4):
            v = g[a, h, 8 * i : 8 * i + 8].astype(F32).reshape(8, 2, 8, DC // 4)
            rows = slice(64 * i, 64 * i + 64)
            pan[a, h, rows, 0 : DC // 4] = v[:, 0].reshape(64, DC // 4).astype(BF16)
            pan[a, h, rows, DC // 4 : DC // 2] = v[:, 1].reshape(64, DC // 4).astype(BF16)

    gather_z(0, 0)
    gather_z(0, 1)
    load("sg", 0, sg_ref, sgt)
    load("su", 1, su_ref, sut)
    load("wg", 2, wg_ref, wga.at[:, 0:FR])
    load("wu", 3, wu_ref, wua.at[:, 0:FR])
    load("lg0", 4, lg_ref, lga.at[0:RANK])
    load("lg1", 5, lg_ref, lga.at[RANK : 2 * RANK])
    load("lu0", 6, lu_ref, lua.at[0:RANK])
    load("lu1", 7, lu_ref, lua.at[RANK : 2 * RANK])
    load("wd", 8, wd_ref, wda.at[0:FR])
    load("ld0", 9, ld_ref, wda.at[FR : FR + RANK])
    load("ld1", 10, ld_ref, wda.at[FR + RANK : FR + 2 * RANK])
    load("sd", 11, sd_ref, sdt)

    rows16 = lax.broadcasted_iota(jnp.int32, (RANK, 128), 0)
    lanes = lax.broadcasted_iota(jnp.int32, (RANK, 128), 1)
    twice = ((lanes % RANK == rows16) & (lanes < 2 * RANK)).astype(F32).astype(BF16)
    for name, src, dst in (("sg", sgt, wga), ("su", sut, wua)):
        loads[name].wait()
        dst[:, FR:FA] = tn(src[...], twice).astype(BF16)
    for dst in (lga, lua):
        dst[2 * RANK : 128] = jnp.zeros((128 - 2 * RANK, FR), BF16)
    wda[FR + 2 * RANK : FA] = jnp.zeros((FA - FR - 2 * RANK, DC), BF16)

    gather_y(0, 0)
    gather_y(0, 1)
    gather_z(1, 0)
    gather_z(1, 1)
    gather_forward(0, 0)
    gather_forward(0, 1)
    loads["sd"].wait()
    sda[...] = tn(sdt[...], twice).astype(BF16)
    gather_y(1, 0)
    gather_y(1, 1)
    for name in ("wg", "wu", "lg0", "lg1", "lu0", "lu1"):
        loads[name].wait()

    other = pl.multiple_of((1 - k) * HALF, HALF)
    mine = pl.multiple_of(k * HALF, HALF)
    myrow = pl.multiple_of(k * HALF + x * QUART, QUART)

    def sum_cores(a):
        send(part.at[a, pl.ds(other, HALF)], sib.at[a], "sib", ("sib", a), dk=1)

    def sum_x(a):
        arrived(sib.at[a], ("sib", a))
        for q in range(NX):
            rows = pl.ds(pl.multiple_of(mine + q * QUART, QUART), QUART)
            v = part[a, rows, :] + sib[a, q * QUART : (q + 1) * QUART, :]
            own[a, q] = v
            xs[a, q] = v.astype(BF16)
        for dx in (1, 3, 2):
            send(xs.at[a, (x + dx) % NX], xr.at[a, dx - 1], "xr", ("xr", a), dx=dx)

    def total_x(a):
        arrived(xr.at[a], ("xr", a))
        return own[a, x] + xr[a, 0].astype(F32) + xr[a, 1].astype(F32) + xr[a, 2].astype(F32)

    low, high = slice(0, DC // 2), slice(DC // 2, DC)
    tiles = [slice(256 * j, 256 * (j + 1)) for j in range(4)]

    def forward_low(a, w):
        for t in tiles:
            acc[a, :, t] = nn(pan[0, 0], w[low, t])

    def forward_high(a, w, lift):
        o = acc[a, :, tiles[3]] + nn(pan[0, 1], w[high, tiles[3]])
        sel = split_inner(o[:, 128:256])
        part[a, :, 768:FR] = o[:, 0:128] + nn(sel, lift[:, 768:FR])
        for t in tiles[:3]:
            part[a, :, t] = acc[a, :, t] + nn(pan[0, 1], w[high, t]) + nn(sel, lift[:, t])

    gather_end(0, 0)
    forward_low(0, wga)
    forward_low(1, wua)
    gather_end(0, 1)
    forward_high(0, wga, lga)
    sum_cores(0)
    forward_high(1, wua, lua)
    sum_cores(1)
    gather_forward(1, 0)
    sum_x(0)
    gather_forward(1, 1)
    sum_x(1)

    for name in ("wd", "ld0", "ld1"):
        loads[name].wait()
    gather_end(1, 0)
    for t in tiles:
        acc[0, :, t] = nt(pan[1, 0], wda[t, low])
    gather_end(1, 1)
    o = acc[0, :, tiles[3]] + nt(pan[1, 1], wda[tiles[3], high])
    sel = split_inner(o[:, 128:256])
    part[2, :, 768:FR] = o[:, 0:128] + nt(sel, sda[768:FR, :])
    for t in tiles[:3]:
        part[2, :, t] = acc[0, :, t] + nt(pan[1, 1], wda[t, high]) + nt(sel, sda[t, :])
    sum_cores(2)

    def spread(a):
        b = act.at[a, pl.ds(myrow, QUART), 0:FR]
        for dx in (1, 3, 2):
            send(b, b, ("a", a), ("ax", a), dx=dx)
        send(b, b, ("a", a), ("ak", a), dk=1)

    def spread_on(a):
        arrived(act.at[a, 0 : 3 * QUART, 0:FR], ("ax", a))
        for dx in (1, 3, 2):
            rows = pl.multiple_of(k * HALF + ((x - dx) % NX) * QUART, QUART)
            b = act.at[a, pl.ds(rows, QUART), 0:FR]
            send(b, b, ("a", a), ("ak", a), dk=1)

    def spread_end(a):
        arrived(act.at[a, 0:HALF, 0:FR], ("ak", a))

    gate = total_x(0)
    up = total_x(1)
    sigmoid = jax.nn.sigmoid(gate)
    act[0, pl.ds(myrow, QUART), 0:FR] = (gate * sigmoid * up).astype(BF16)
    spread(0)

    def at_y(d):
        return pl.ds(pl.multiple_of(((y + d) % NY) * TY, TY), TY)

    def parts_of(j):
        return slice(CW * j, CW * j + CW // 2), slice(CW * j + CW // 2, CW * (j + 1))

    def y_send(a, j, value):
        mf[a, :, CW * j : CW * (j + 1)] = value
        for h, part_cols in enumerate(parts_of(0)):
            ms[a, 2 * j + h] = value[:, part_cols].astype(BF16)
        first, rest = ms.at[a, 2 * j], ms.at[a, 2 * j + 1]
        if (a, j) in RS_DIRECT:
            for h in range(2):
                for i, dy in enumerate((1, 3)):
                    send(ms.at[a, 2 * j + h, at_y(dy)], ry.at[a, j, i, h], ("y", a), ("ry", a, j), dy=dy)
            for h in range(2):
                send(ms.at[a, 2 * j + h, at_y(2)], rp.at[a, j, h], ("y", a), ("rp", a, j), dy=2)
            return
        send(first.at[at_y(2)], rp.at[a, j, 0], ("y", a), ("rp", a, j), dy=1)
        send(rest.at[at_y(2)], rp.at[a, j, 1], ("y", a), ("rp", a, j), dy=3)
        send(rest.at[at_y(1)], ry.at[a, j, 0, 1], ("y", a), ("ry", a, j), dy=1)
        send(first.at[at_y(3)], ry.at[a, j, 1, 0], ("y", a), ("ry", a, j), dy=3)

    def y_relay(a, j):
        if (a, j) in RS_DIRECT:
            return
        arrived(rp.at[a, j], ("rp", a, j))
        for i, (dy, cols) in enumerate(zip((1, 3), parts_of(j))):
            b = ms.at[a, 2 * j + i, at_y(dy)]
            b[...] = (mf[a, at_y(dy), cols] + rp[a, j, i].astype(F32)).astype(BF16)
            send(b, ry.at[a, j, i, i], ("y", a), ("ry", a, j), dy=dy)

    def z_send(a, j):
        arrived(ry.at[a, j], ("ry", a, j))
        w = ry[a, j, 0].astype(F32) + ry[a, j, 1].astype(F32)
        if (a, j) in RS_DIRECT:
            arrived(rp.at[a, j], ("rp", a, j))
            w = w + rp[a, j].astype(F32)
        v = mf[a, at_y(0), CW * j : CW * (j + 1)] + jnp.concatenate([w[0], w[1]], axis=1)
        v = v.reshape(NZ, 8, CW)
        v = jnp.concatenate([v[:, :, : CW // 2], v[:, :, CW // 2 :]], axis=1)
        zo[a, j] = v
        zs[a, j] = v.astype(BF16)
        for dz in (4, 3, 5, 2, 6, 1, 7):
            send(zs.at[a, j, (z + dz) % NZ], zr.at[a, j, dz - 1], ("z", a), ("zr", a, j), dz=dz)

    def z_end(a, j, out_ref):
        v = zo[a, j, z]
        arrived(zr.at[a, j], ("zr", a, j))
        for dz in range(1, NZ):
            v = v + zr[a, j, dz - 1].astype(F32)
        first, rest = parts_of(j)
        out_ref[:, first] = v[0:8].astype(BF16)
        out_ref[:, rest] = v[8:16].astype(BF16)

    def down(j):
        y_send(0, j, nn(act[0], wda[:, CW * j : CW * (j + 1)]))

    def back(j):
        rows = slice(CW * j, CW * (j + 1))
        y_send(1, j, nt(act[1], wga[rows, :]) + nt(act[2], wua[rows, :]))

    sum_x(2)
    spread_on(0)

    hidden_gradient = total_x(2)
    act[1, pl.ds(myrow, QUART), 0:FR] = (
        hidden_gradient * up * sigmoid * (1.0 + gate * (1.0 - sigmoid))
    ).astype(BF16)
    act[2, pl.ds(myrow, QUART), 0:FR] = (hidden_gradient * gate * sigmoid).astype(BF16)
    spread(1)
    spread(2)

    spread_end(0)
    act[0, :, FR:FA] = split_inner(nn(act[0, :, 0:FR], sda[...]))
    down(0)
    down(1)
    down(2)
    spread_on(1)
    y_relay(0, 0)
    down(3)
    spread_on(2)
    y_relay(0, 1)
    y_relay(0, 2)
    z_send(0, 0)
    y_relay(0, 3)
    z_send(0, 1)
    spread_end(1)
    act[1, :, FR:FA] = split_inner(nt(act[1, :, 0:FR], lga[...]))
    spread_end(2)
    act[2, :, FR:FA] = split_inner(nt(act[2, :, 0:FR], lua[...]))
    back(0)
    z_send(0, 2)
    back(1)
    y_relay(1, 0)
    z_send(0, 3)
    back(2)
    y_relay(1, 1)
    back(3)
    y_relay(1, 2)
    z_send(1, 0)
    y_relay(1, 3)
    z_send(1, 1)
    for j in range(NCH):
        z_end(0, j, mixed_ref)
    z_send(1, 2)
    z_send(1, 3)
    for j in range(NCH):
        z_end(1, j, tg_ref)
    for a in range(2):
        for h in range(2):
            all_sent(g.at[a, h, 0:31], ("g", a, h))
    all_sent(sib, "sib")
    all_sent(xr, "xr")
    for a in range(3):
        all_sent(act.at[a, 0 : 7 * QUART, 0:FR], ("a", a))
    for a in range(2):
        all_sent(ms.at[a, 0:6], ("y", a))
        all_sent(zr.at[a], ("z", a))


def hand_over(mixed_ref, tg_ref, mixed_out, tg_out):
    mixed_out[...] = mixed_ref[...]
    tg_out[...] = tg_ref[...]


def on_device(tokens, gate_w, up_w, down_w, gate_s, gate_l, up_s, up_l, down_s, down_l, cotangent):
    vmem = pl.BlockSpec(memory_space=pltpu.VMEM)
    anywhere = pl.BlockSpec(memory_space=pl.ANY)
    out = jax.ShapeDtypeStruct((T // NY // NZ, DC), BF16)
    mixed, gradient = pl.pallas_call(
        kernel,
        out_shape=(out, out),
        in_specs=[anywhere] * 11,
        out_specs=(vmem, vmem),
        scratch_shapes=[
            pltpu.VMEM((2, T // NY // NZ, DC), BF16),
            pltpu.VMEM((DC, FA), BF16),
            pltpu.VMEM((DC, FA), BF16),
            pltpu.VMEM((FA, DC), BF16),
            pltpu.VMEM((128, FR), BF16),
            pltpu.VMEM((128, FR), BF16),
            pltpu.VMEM((FR, 128), BF16),
            pltpu.VMEM((RANK, DC), BF16),
            pltpu.VMEM((RANK, DC), BF16),
            pltpu.VMEM((RANK, FR), BF16),
            pltpu.VMEM((2, 2, NY * NZ, 16, DC // 4), BF16),
            pltpu.VMEM((2, 2, T, DC // 2), BF16),
            pltpu.VMEM((2, T, FA), F32),
            pltpu.VMEM((3, T, FR), F32),
            pltpu.VMEM((3, HALF, FR), F32),
            pltpu.VMEM((3, NX, QUART, FR), F32),
            pltpu.VMEM((3, NX, QUART, FR), BF16),
            pltpu.VMEM((3, NX - 1, QUART, FR), BF16),
            pltpu.VMEM((3, T, FA), BF16),
            pltpu.VMEM((2, T, DC), F32),
            pltpu.VMEM((2, 2 * NCH, T, CW // 2), BF16),
            pltpu.VMEM((2, NCH, 2, 2, TY, CW // 2), BF16),
            pltpu.VMEM((2, NCH, 2, TY, CW // 2), BF16),
            pltpu.VMEM((2, NCH, NZ, 16, CW // 2), F32),
            pltpu.VMEM((2, NCH, NZ, 16, CW // 2), BF16),
            pltpu.VMEM((2, NCH, NZ - 1, 16, CW // 2), BF16),
            pltpu.SemaphoreType.DMA((14,)),
            pltpu.SemaphoreType.DMA((13,)),
            pltpu.SemaphoreType.DMA((72,)),
        ],
        compiler_params=pltpu.CompilerParams(
            collective_id=0, has_side_effects=True, vmem_limit_bytes=58 * 2**20
        ),
        name="lora_swiglu",
    )(tokens, cotangent, gate_w, up_w, down_w, gate_s.T, gate_l, up_s.T, up_l, down_s.T, down_l)
    return pl.pallas_call(
        hand_over, out_shape=(out, out), in_specs=[vmem] * 2, out_specs=(vmem, vmem), name="hand_over"
    )(mixed, gradient)


def solution(mesh):
    placed = (
        P("row", "col"),
        P("col", "row"),
        P("col", "row"),
        P("row", "col"),
        P("col", None),
        P(None, "row"),
        P("col", None),
        P(None, "row"),
        P("row", None),
        P(None, "col"),
        P("row", "col"),
    )
    return jax.shard_map(
        on_device,
        mesh=mesh,
        in_specs=placed,
        out_specs=(P("row", "col"), P("row", "col")),
        check_vma=False,
    )
```

```python
import jax
import jax.numpy as jnp
from jax import lax
from jax.experimental import pallas as pl
from jax.experimental.pallas import tpu as pltpu
from jax.sharding import PartitionSpec as P

MESH = pl.DeviceIdType.MESH
F32, BF16 = jnp.float32, jnp.bfloat16

NX, NCORE, NY, NZ = 4, 2, 4, 8
T, DC, FR, RANK = 256, 2048, 896, 16
FA = 1024
HALF, QUART = T // NCORE, T // NCORE // NX
TY = T // NY
CW = 512
NCH = DC // CW
ZGROUPS = ((0,), (1, 7), (2, 6), (3, 5, 4))
SCALE = 0.5
RS_DIRECT = ((1, 2), (1, 3))


def nn(a, b):
    return jnp.dot(a, b, preferred_element_type=F32)


def nt(a, b):
    return lax.dot_general(a, b, (((1,), (1,)), ((), ())), preferred_element_type=F32)


def tn(a, b):
    return lax.dot_general(a, b, (((0,), (0,)), ((), ())), preferred_element_type=F32)


def split_inner(inner):
    top = inner.astype(BF16).astype(F32)
    lane = lax.broadcasted_iota(jnp.int32, inner.shape, 1)
    return (jnp.where(lane < RANK, top, inner - top) * SCALE).astype(BF16)


def kernel(
    x_ref, dy_ref, wg_ref, wu_ref, wd_ref, sg_ref, lg_ref, su_ref, lu_ref, sd_ref, ld_ref,
    mixed_ref, tg_ref,
    xin, wga, wua, wda, lga, lua, sda, sgt, sut, sdt,
    g, pan, acc, part, sib, own, xs, xr, act, mf, ms, ry, rp, zo, zs, zr,
    wsem, ss, rs,
):
    r, c = lax.axis_index("row"), lax.axis_index("col")
    y, z = r // NZ, r % NZ
    x, k = c // NCORE, c % NCORE

    def dev(dx=0, dk=0, dy=0, dz=0):
        return {
            "row": ((y + dy) % NY) * NZ + (z + dz) % NZ,
            "col": ((x + dx) % NX) * NCORE + (k + dk) % NCORE,
        }

    peers = (
        [dict(dz=d) for d in range(1, NZ)]
        + [dict(dy=d) for d in range(1, NY)]
        + [dict(dx=d) for d in range(1, NX)]
        + [dict(dk=1)]
    )
    barrier = pltpu.get_barrier_semaphore()
    for p in peers:
        pl.semaphore_signal(barrier, inc=1, device_id=dev(**p), device_id_type=MESH)

    loads = {}

    def load(name, i, src, dst):
        cp = pltpu.make_async_copy(src, dst, wsem.at[i])
        cp.start()
        loads[name] = cp

    load("x", 12, x_ref, xin.at[0])
    load("dy", 13, dy_ref, xin.at[1])
    loads["x"].wait()
    loads["dy"].wait()

    for a in range(2):
        v = xin[a].astype(F32)
        for h in range(2):
            q = DC // 4
            g[a, h, r] = jnp.concatenate(
                [v[:, 2 * h * q : (2 * h + 1) * q], v[:, (2 * h + 1) * q : (2 * h + 2) * q]], axis=0
            ).astype(BF16)

    pl.semaphore_wait(barrier, len(peers))

    recv_sems, send_sems = {}, {}

    def sem_of(ref, table, key):
        return ref.at[table.setdefault(key, len(table))]

    def send(src, dst, sent, key, **to):
        cp = pltpu.make_async_remote_copy(
            src_ref=src, dst_ref=dst, send_sem=sem_of(ss, send_sems, sent), recv_sem=sem_of(rs, recv_sems, key),
            device_id=dev(**to), device_id_type=MESH,
        )
        cp.start()

    def arrived(like, key):
        pltpu.make_async_remote_copy(
            src_ref=like, dst_ref=like, send_sem=ss.at[0], recv_sem=sem_of(rs, recv_sems, key),
            device_id=dev(dk=1), device_id_type=MESH,
        ).wait_recv()

    def all_sent(like, sent):
        pltpu.make_async_remote_copy(
            src_ref=like, dst_ref=like, send_sem=sem_of(ss, send_sems, sent), recv_sem=rs.at[0],
            device_id=dev(dk=1), device_id_type=MESH,
        ).wait_send()

    def block(a, h, dy, dz):
        return g.at[a, h, ((y + dy) % NY) * NZ + (z + dz) % NZ]

    def gather_z(a, h):
        b = block(a, h, 0, 0)
        for i, group in enumerate(ZGROUPS[1:]):
            for dz in group:
                send(b, b, ("g", a, h), ("gz", a, h, i + 1), dz=dz)

    def gather_y(a, h):
        for i, group in enumerate(ZGROUPS):
            if i:
                arrived(g.at[a, h, 0 : len(group)], ("gz", a, h, i))
            for dz in group:
                b = block(a, h, 0, -dz)
                send(b, b, ("g", a, h), ("gy", a, h, i), dy=(1, 3)[h])
                send(b, b, ("g", a, h), ("ge", a, h), dy=(3, 1)[h])

    def gather_forward(a, h):
        dy = (1, 3)[h]
        for i, group in enumerate(ZGROUPS):
            arrived(g.at[a, h, 0 : len(group)], ("gy", a, h, i))
            for dz in group:
                b = block(a, h, -dy, -dz)
                send(b, b, ("g", a, h), ("gf", a, h), dy=dy)

    def gather_end(a, h):
        arrived(g.at[a, h, 0:NZ], ("ge", a, h))
        arrived(g.at[a, h, 0:NZ], ("gf", a, h))
        for i in range(4):
            v = g[a, h, 8 * i : 8 * i + 8].astype(F32).reshape(8, 2, 8, DC // 4)
            rows = slice(64 * i, 64 * i + 64)
            pan[a, h, rows, 0 : DC // 4] = v[:, 0].reshape(64, DC // 4).astype(BF16)
            pan[a, h, rows, DC // 4 : DC // 2] = v[:, 1].reshape(64, DC // 4).astype(BF16)

    gather_z(0, 0)
    gather_z(0, 1)
    load("sg", 0, sg_ref, sgt)
    load("su", 1, su_ref, sut)
    load("wg", 2, wg_ref, wga.at[:, 0:FR])
    load("wu", 3, wu_ref, wua.at[:, 0:FR])
    load("lg0", 4, lg_ref, lga.at[0:RANK])
    load("lg1", 5, lg_ref, lga.at[RANK : 2 * RANK])
    load("lu0", 6, lu_ref, lua.at[0:RANK])
    load("lu1", 7, lu_ref, lua.at[RANK : 2 * RANK])
    load("wd", 8, wd_ref, wda.at[0:FR])
    load("ld0", 9, ld_ref, wda.at[FR : FR + RANK])
    load("ld1", 10, ld_ref, wda.at[FR + RANK : FR + 2 * RANK])
    load("sd", 11, sd_ref, sdt)

    rows16 = lax.broadcasted_iota(jnp.int32, (RANK, 128), 0)
    lanes = lax.broadcasted_iota(jnp.int32, (RANK, 128), 1)
    twice = ((lanes % RANK == rows16) & (lanes < 2 * RANK)).astype(F32).astype(BF16)
    for name, src, dst in (("sg", sgt, wga), ("su", sut, wua)):
        loads[name].wait()
        dst[:, FR:FA] = tn(src[...], twice).astype(BF16)
    for dst in (lga, lua):
        dst[2 * RANK : 128] = jnp.zeros((128 - 2 * RANK, FR), BF16)
    wda[FR + 2 * RANK : FA] = jnp.zeros((FA - FR - 2 * RANK, DC), BF16)

    gather_y(0, 0)
    gather_y(0, 1)
    gather_z(1, 0)
    gather_z(1, 1)
    gather_forward(0, 0)
    gather_forward(0, 1)
    loads["sd"].wait()
    sda[...] = tn(sdt[...], twice).astype(BF16)
    gather_y(1, 0)
    gather_y(1, 1)
    for name in ("wg", "wu", "lg0", "lg1", "lu0", "lu1"):
        loads[name].wait()

    other = pl.multiple_of((1 - k) * HALF, HALF)
    mine = pl.multiple_of(k * HALF, HALF)
    myrow = pl.multiple_of(k * HALF + x * QUART, QUART)

    def sum_cores(a):
        send(part.at[a, pl.ds(other, HALF)], sib.at[a], "sib", ("sib", a), dk=1)

    def sum_x(a):
        arrived(sib.at[a], ("sib", a))
        for q in range(NX):
            rows = pl.ds(pl.multiple_of(mine + q * QUART, QUART), QUART)
            v = part[a, rows, :] + sib[a, q * QUART : (q + 1) * QUART, :]
            own[a, q] = v
            xs[a, q] = v.astype(BF16)
        for dx in (1, 3, 2):
            send(xs.at[a, (x + dx) % NX], xr.at[a, dx - 1], "xr", ("xr", a), dx=dx)

    def total_x(a):
        arrived(xr.at[a], ("xr", a))
        return own[a, x] + xr[a, 0].astype(F32) + xr[a, 1].astype(F32) + xr[a, 2].astype(F32)

    low, high = slice(0, DC // 2), slice(DC // 2, DC)
    tiles = [slice(256 * j, 256 * (j + 1)) for j in range(4)]

    def forward_low(a, w):
        for t in tiles:
            acc[a, :, t] = nn(pan[0, 0], w[low, t])

    def forward_high(a, w, lift):
        o = acc[a, :, tiles[3]] + nn(pan[0, 1], w[high, tiles[3]])
        sel = split_inner(o[:, 128:256])
        part[a, :, 768:FR] = o[:, 0:128] + nn(sel, lift[:, 768:FR])
        for t in tiles[:3]:
            part[a, :, t] = acc[a, :, t] + nn(pan[0, 1], w[high, t]) + nn(sel, lift[:, t])

    gather_end(0, 0)
    forward_low(0, wga)
    forward_low(1, wua)
    gather_end(0, 1)
    forward_high(0, wga, lga)
    sum_cores(0)
    forward_high(1, wua, lua)
    sum_cores(1)
    sum_x(0)
    sum_x(1)
    gather_forward(1, 0)
    gather_forward(1, 1)

    for name in ("wd", "ld0", "ld1"):
        loads[name].wait()
    gather_end(1, 0)
    for t in tiles:
        acc[0, :, t] = nt(pan[1, 0], wda[t, low])
    gather_end(1, 1)
    o = acc[0, :, tiles[3]] + nt(pan[1, 1], wda[tiles[3], high])
    sel = split_inner(o[:, 128:256])
    part[2, :, 768:FR] = o[:, 0:128] + nt(sel, sda[768:FR, :])
    for t in tiles[:3]:
        part[2, :, t] = acc[0, :, t] + nt(pan[1, 1], wda[t, high]) + nt(sel, sda[t, :])
    sum_cores(2)

    def spread(a):
        b = act.at[a, pl.ds(myrow, QUART), 0:FR]
        for dx in (1, 3, 2):
            send(b, b, ("a", a), ("ax", a), dx=dx)
        send(b, b, ("a", a), ("ak", a), dk=1)

    def spread_on(a):
        arrived(act.at[a, 0 : 3 * QUART, 0:FR], ("ax", a))
        for dx in (1, 3, 2):
            rows = pl.multiple_of(k * HALF + ((x - dx) % NX) * QUART, QUART)
            b = act.at[a, pl.ds(rows, QUART), 0:FR]
            send(b, b, ("a", a), ("ak", a), dk=1)

    def spread_end(a):
        arrived(act.at[a, 0:HALF, 0:FR], ("ak", a))

    gate = total_x(0)
    up = total_x(1)
    sigmoid = jax.nn.sigmoid(gate)
    act[0, pl.ds(myrow, QUART), 0:FR] = (gate * sigmoid * up).astype(BF16)
    spread(0)

    def at_y(d):
        return pl.ds(pl.multiple_of(((y + d) % NY) * TY, TY), TY)

    def parts_of(j):
        return slice(CW * j, CW * j + CW // 2), slice(CW * j + CW // 2, CW * (j + 1))

    def y_send(a, j, value):
        mf[a, :, CW * j : CW * (j + 1)] = value
        for h, part_cols in enumerate(parts_of(0)):
            ms[a, 2 * j + h] = value[:, part_cols].astype(BF16)
        first, rest = ms.at[a, 2 * j], ms.at[a, 2 * j + 1]
        if (a, j) in RS_DIRECT:
            for h in range(2):
                for i, dy in enumerate((1, 3)):
                    send(ms.at[a, 2 * j + h, at_y(dy)], ry.at[a, j, i, h], ("y", a), ("ry", a, j), dy=dy)
            for h in range(2):
                send(ms.at[a, 2 * j + h, at_y(2)], rp.at[a, j, h], ("y", a), ("rp", a, j), dy=2)
            return
        send(first.at[at_y(2)], rp.at[a, j, 0], ("y", a), ("rp", a, j), dy=1)
        send(rest.at[at_y(2)], rp.at[a, j, 1], ("y", a), ("rp", a, j), dy=3)
        send(rest.at[at_y(1)], ry.at[a, j, 0, 1], ("y", a), ("ry", a, j), dy=1)
        send(first.at[at_y(3)], ry.at[a, j, 1, 0], ("y", a), ("ry", a, j), dy=3)

    def y_relay(a, j):
        if (a, j) in RS_DIRECT:
            return
        arrived(rp.at[a, j], ("rp", a, j))
        for i, (dy, cols) in enumerate(zip((1, 3), parts_of(j))):
            b = ms.at[a, 2 * j + i, at_y(dy)]
            b[...] = (mf[a, at_y(dy), cols] + rp[a, j, i].astype(F32)).astype(BF16)
            send(b, ry.at[a, j, i, i], ("y", a), ("ry", a, j), dy=dy)

    def z_send(a, j):
        arrived(ry.at[a, j], ("ry", a, j))
        w = ry[a, j, 0].astype(F32) + ry[a, j, 1].astype(F32)
        if (a, j) in RS_DIRECT:
            arrived(rp.at[a, j], ("rp", a, j))
            w = w + rp[a, j].astype(F32)
        v = mf[a, at_y(0), CW * j : CW * (j + 1)] + jnp.concatenate([w[0], w[1]], axis=1)
        v = v.reshape(NZ, 8, CW)
        v = jnp.concatenate([v[:, :, : CW // 2], v[:, :, CW // 2 :]], axis=1)
        zo[a, j] = v
        zs[a, j] = v.astype(BF16)
        for dz in (4, 3, 5, 2, 6, 1, 7):
            send(zs.at[a, j, (z + dz) % NZ], zr.at[a, j, dz - 1], ("z", a), ("zr", a, j), dz=dz)

    def z_end(a, j, out_ref):
        v = zo[a, j, z]
        arrived(zr.at[a, j], ("zr", a, j))
        for dz in range(1, NZ):
            v = v + zr[a, j, dz - 1].astype(F32)
        first, rest = parts_of(j)
        out_ref[:, first] = v[0:8].astype(BF16)
        out_ref[:, rest] = v[8:16].astype(BF16)

    def down(j):
        y_send(0, j, nn(act[0], wda[:, CW * j : CW * (j + 1)]))

    def back(j):
        rows = slice(CW * j, CW * (j + 1))
        y_send(1, j, nt(act[1], wga[rows, :]) + nt(act[2], wua[rows, :]))

    sum_x(2)
    spread_on(0)

    hidden_gradient = total_x(2)
    act[1, pl.ds(myrow, QUART), 0:FR] = (
        hidden_gradient * up * sigmoid * (1.0 + gate * (1.0 - sigmoid))
    ).astype(BF16)
    act[2, pl.ds(myrow, QUART), 0:FR] = (hidden_gradient * gate * sigmoid).astype(BF16)
    spread(1)
    spread(2)

    spread_end(0)
    act[0, :, FR:FA] = split_inner(nn(act[0, :, 0:FR], sda[...]))
    down(0)
    down(1)
    down(2)
    spread_on(1)
    y_relay(0, 0)
    down(3)
    spread_on(2)
    y_relay(0, 1)
    y_relay(0, 2)
    z_send(0, 0)
    y_relay(0, 3)
    z_send(0, 1)
    spread_end(1)
    act[1, :, FR:FA] = split_inner(nt(act[1, :, 0:FR], lga[...]))
    spread_end(2)
    act[2, :, FR:FA] = split_inner(nt(act[2, :, 0:FR], lua[...]))
    back(0)
    z_send(0, 2)
    back(1)
    y_relay(1, 0)
    z_send(0, 3)
    back(2)
    y_relay(1, 1)
    back(3)
    y_relay(1, 2)
    z_send(1, 0)
    y_relay(1, 3)
    z_send(1, 1)
    for j in range(NCH):
        z_end(0, j, mixed_ref)
    z_send(1, 2)
    z_send(1, 3)
    for j in range(NCH):
        z_end(1, j, tg_ref)
    for a in range(2):
        for h in range(2):
            all_sent(g.at[a, h, 0:31], ("g", a, h))
    all_sent(sib, "sib")
    all_sent(xr, "xr")
    for a in range(3):
        all_sent(act.at[a, 0 : 7 * QUART, 0:FR], ("a", a))
    for a in range(2):
        all_sent(ms.at[a, 0:6], ("y", a))
        all_sent(zr.at[a], ("z", a))


def hand_over(mixed_ref, tg_ref, mixed_out, tg_out):
    mixed_out[...] = mixed_ref[...]
    tg_out[...] = tg_ref[...]


def on_device(tokens, gate_w, up_w, down_w, gate_s, gate_l, up_s, up_l, down_s, down_l, cotangent):
    vmem = pl.BlockSpec(memory_space=pltpu.VMEM)
    anywhere = pl.BlockSpec(memory_space=pl.ANY)
    out = jax.ShapeDtypeStruct((T // NY // NZ, DC), BF16)
    mixed, gradient = pl.pallas_call(
        kernel,
        out_shape=(out, out),
        in_specs=[anywhere] * 11,
        out_specs=(vmem, vmem),
        scratch_shapes=[
            pltpu.VMEM((2, T // NY // NZ, DC), BF16),
            pltpu.VMEM((DC, FA), BF16),
            pltpu.VMEM((DC, FA), BF16),
            pltpu.VMEM((FA, DC), BF16),
            pltpu.VMEM((128, FR), BF16),
            pltpu.VMEM((128, FR), BF16),
            pltpu.VMEM((FR, 128), BF16),
            pltpu.VMEM((RANK, DC), BF16),
            pltpu.VMEM((RANK, DC), BF16),
            pltpu.VMEM((RANK, FR), BF16),
            pltpu.VMEM((2, 2, NY * NZ, 16, DC // 4), BF16),
            pltpu.VMEM((2, 2, T, DC // 2), BF16),
            pltpu.VMEM((2, T, FA), F32),
            pltpu.VMEM((3, T, FR), F32),
            pltpu.VMEM((3, HALF, FR), F32),
            pltpu.VMEM((3, NX, QUART, FR), F32),
            pltpu.VMEM((3, NX, QUART, FR), BF16),
            pltpu.VMEM((3, NX - 1, QUART, FR), BF16),
            pltpu.VMEM((3, T, FA), BF16),
            pltpu.VMEM((2, T, DC), F32),
            pltpu.VMEM((2, 2 * NCH, T, CW // 2), BF16),
            pltpu.VMEM((2, NCH, 2, 2, TY, CW // 2), BF16),
            pltpu.VMEM((2, NCH, 2, TY, CW // 2), BF16),
            pltpu.VMEM((2, NCH, NZ, 16, CW // 2), F32),
            pltpu.VMEM((2, NCH, NZ, 16, CW // 2), BF16),
            pltpu.VMEM((2, NCH, NZ - 1, 16, CW // 2), BF16),
            pltpu.SemaphoreType.DMA((14,)),
            pltpu.SemaphoreType.DMA((13,)),
            pltpu.SemaphoreType.DMA((72,)),
        ],
        compiler_params=pltpu.CompilerParams(
            collective_id=0, has_side_effects=True, vmem_limit_bytes=58 * 2**20
        ),
        name="lora_swiglu",
    )(tokens, cotangent, gate_w, up_w, down_w, gate_s.T, gate_l, up_s.T, up_l, down_s.T, down_l)
    return pl.pallas_call(
        hand_over, out_shape=(out, out), in_specs=[vmem] * 2, out_specs=(vmem, vmem), name="hand_over"
    )(mixed, gradient)


def solution(mesh):
    placed = (
        P("row", "col"),
        P("col", "row"),
        P("col", "row"),
        P("row", "col"),
        P("col", None),
        P(None, "row"),
        P("col", None),
        P(None, "row"),
        P("row", None),
        P(None, "col"),
        P("row", "col"),
    )
    return jax.shard_map(
        on_device,
        mesh=mesh,
        in_specs=placed,
        out_specs=(P("row", "col"), P("row", "col")),
        check_vma=False,
    )
```
